32 devices in a mesh: lon: 8 (over z, y), lat: 4 (over x, core).
Axes of the slice: x: 2, y: 2, z: 4, core: 2. Of those that a mesh axis runs over, the one named last changes fastest.
Arguments:
- adjoint_final: float32 [10, 256, 2048], P(None, 'lat', 'lon'), may hold values from -6 to 6
- stored_tracer: float32 [4, 10, 256, 2048], P(None, None, 'lat', 'lon'), may hold values from -4 to 4
- stored_zonal: float32 [4, 10, 256, 2048], P(None, None, 'lat', 'lon'), may hold values from -4 to 4
- stored_meridional: float32 [4, 10, 256, 2048], P(None, None, 'lat', 'lon'), may hold values from -4 to 4
- diffusivity: float32 [256, 2048], P('lat', 'lon'), may hold values from 0.02 to 0.2
- level_mixing: float32 [10, 10], replicated, may hold values from -2 to 2
- wet_tiles: int32 [4, 16], P('lat', 'lon'), may hold values 0 or 1
- state_index: int32 [2], replicated, may hold values from 0 to 3, as said below
Outputs:
- adjoint_start: float32 [10, 256, 2048], P(None, 'lat', 'lon')
The draws below stay inside these ranges and needn't reach their ends.
Inputs may be any that keep to these rules, and one draw needn't show every extreme that they name: The entries of state_index are distinct stored states, and one of them is the last stored state.
All inputs are finite; a program needn't handle non-finite values. No bound on the sum of `wet_tiles` on one device may be relied on, other than what follows from the above.
Results may differ from the reference program's by a relative error of at most 0.0001.
Values sent between devices are 32-bit elements; how exact they have to be, the bound alone decides.
A program may use at most 64 MiB of HBM per device.

```python
import math
import jax
import jax.numpy as jnp
from jax import lax

LEV = 10
TLAT = 64
TLON = 128
STEPS = 2
STORE = 4
NLON = 2048
NLAT = 256
NTLON = 16
N_LAT = 4


def draw_state_index(key, part):
    others = jax.random.permutation(jax.random.fold_in(key, 11), STORE - 1)[:STEPS - 1].astype(jnp.int32)
    values = jnp.concatenate([others, jnp.full((1,), STORE - 1, jnp.int32)])
    order = jax.random.permutation(jax.random.fold_in(key, 13), STEPS)
    return values[order].astype(jnp.int32)


def with_ends(array, own_key, least, high):
    place = [jax.random.randint(jax.random.fold_in(own_key, axis), (), 0, length) for axis, length in enumerate(array.shape)]
    widest = array.shape.index(max(array.shape))
    next_to = place[:widest] + [(place[widest] + 1) % array.shape[widest]] + place[widest + 1:]
    return array.at[tuple(place)].set(least).at[tuple(next_to)].set(high)


def shard_levels(stream_key, shape, pieces, low, top_value):
    def one(dim, shards_of):
        steps = jax.random.uniform(jax.random.fold_in(jax.random.fold_in(stream_key, 6), dim), (shards_of,), jnp.float32, low / len(pieces), top_value / len(pieces))
        return jnp.repeat(jnp.exp(steps), shape[dim] // shards_of).reshape((-1,) + (1,) * (len(shape) - dim - 1))

    factor_of = one(*pieces[0])
    for cut in pieces[1:]:
        factor_of = factor_of * one(*cut)
    return factor_of


def scatter_about(key, extent, scale, limit, shards=(), kind=jnp.bfloat16):
    factor_of = shard_levels(key, extent, shards, -0.22, 0.18) if shards else 1.0
    array = jax.random.normal(key, extent, jnp.float32) * scale * factor_of
    return jnp.minimum(jnp.maximum(array, -limit), limit).astype(kind)


def setup_inputs(seed: int = 0) -> dict:
    seeds = jax.random.split(jax.random.key(seed), 9)
    return {
        "adjoint_final": scatter_about(seeds[0], (LEV, NLAT, NLON), 1.0, 6.0, ((1, 4), (2, 8)), jnp.float32),
        "stored_tracer": scatter_about(seeds[1], (STORE, LEV, NLAT, NLON), 1.0, 4.0, ((2, 4), (3, 8)), jnp.float32),
        "stored_zonal": scatter_about(seeds[2], (STORE, LEV, NLAT, NLON), 1.0, 4.0, ((2, 4), (3, 8)), jnp.float32),
        "stored_meridional": scatter_about(seeds[3], (STORE, LEV, NLAT, NLON), 1.0, 4.0, ((2, 4), (3, 8)), jnp.float32),
        "diffusivity": jnp.clip(jnp.exp(math.log(0.2) - 2.3025851 * jax.random.uniform(seeds[4], (NLAT, NLON), jnp.float32) ** shard_levels(seeds[4], (NLAT, NLON), ((0, 4), (1, 8)), -0.2, 0.2)), 0.02, 0.2),
        "level_mixing": scatter_about(seeds[5], (LEV, LEV), LEV ** -0.5, 2.0, (), jnp.float32),
        "wet_tiles": with_ends((jax.random.randint(seeds[6], (N_LAT, NTLON), 0, 4) < 3).astype(jnp.int32), jax.random.fold_in(seeds[6], 1), 0, 1),
        "state_index": draw_state_index(jax.random.fold_in(seeds[8], 71), 0),
    }


advect_scale = 0.25
damping = 0.3


def east_of(field):
    return jnp.roll(field, -1, 2)


def west_of(field):
    return jnp.roll(field, 1, 2)


def north_of(field):
    return jnp.concatenate([field[:, 1:, :], field[:, -1:, ::-1]], axis=1)


def south_of(field):
    return jnp.concatenate([jnp.zeros_like(field[:, :1, :]), field[:, :-1, :]], axis=1)


def reference(adjoint_final, stored_tracer, stored_zonal, stored_meridional, diffusivity, level_mixing, wet_tiles, state_index):
    wet = jnp.repeat(jnp.repeat(wet_tiles, TLAT, 0), TLON, 1).astype(jnp.float32)[None]
    adjoint = adjoint_final * wet
    for back in range(STEPS):
        chosen = state_index[STEPS - 1 - back]
        tracer = stored_tracer[chosen]
        zonal = stored_zonal[chosen]
        merid = stored_meridional[chosen]
        spread = diffusivity[None] * adjoint
        zonal_flux = zonal * adjoint
        merid_flux = merid * adjoint
        nearby = east_of(spread) + west_of(spread) + north_of(spread) + south_of(spread)
        advect = east_of(zonal_flux) - west_of(zonal_flux) + north_of(merid_flux) - south_of(merid_flux)
        vertical = jnp.einsum("ml,mab->lab", level_mixing, adjoint, precision=lax.Precision.HIGHEST)
        adjoint = wet * (adjoint - 4.0 * spread + nearby + advect_scale * advect + vertical - damping * tracer * tracer * adjoint)
    return adjoint
```

```python
import functools

import jax
import jax.numpy as jnp
from jax import lax
from jax.experimental import pallas as pl
from jax.experimental.pallas import tpu as pltpu
from jax.sharding import PartitionSpec as P

TLON = 128
STEPS = 2
LANES = 128
ROWS = 8

advect_scale = 0.25
damping = 0.3

MESH = pl.DeviceIdType.MESH


def kernel(
    lons, lats,
    af_h, q_h, u_h, v_h, d_h, mix, wet, sidx,
    out,
    af, q, u, v, dv, mid, wbuf, col_out, col_in, row_out, row_in,
    load_sem, send_sem, recv_sem,
):
    levels, height, width = af.shape
    store = u.shape[0]
    strips = height // ROWS
    pitch = LANES // strips
    lon = lax.axis_index("lon")
    lat = lax.axis_index("lat")
    east = lax.rem(lon + 1, lons)
    west = lax.rem(lon + lons - 1, lons)
    mirror = lons - 1 - lon
    top = lats - 1

    barrier = pltpu.get_barrier_semaphore()

    def greet(device_id):
        pl.semaphore_signal(barrier, inc=1, device_id=device_id, device_id_type=MESH)

    greet({"lon": east})
    greet({"lon": west})

    @pl.when(lat < top)
    def _():
        greet({"lat": lat + 1})

    folds = (lat == top) & (mirror != east) & (mirror != west)
    four = ((lat > 0) & (lat < top)) | folds

    @pl.when(folds)
    def _():
        greet({"lon": mirror})

    @pl.when(lat > 0)
    def _():
        greet({"lat": lat - 1})

    loads = [(d_h, dv), (af_h, af)]
    loads += [(u_h.at[s], u.at[s]) for s in range(store)]
    loads += [(v_h.at[s], v.at[s]) for s in range(store)]
    loads += [(q_h.at[s], q.at[s]) for s in range(store)]
    loads = [pltpu.make_async_copy(src, dst, load_sem.at[i]) for i, (src, dst) in enumerate(loads)]
    for load in loads:
        load.start()

    for t in range(width // TLON):
        flag = wet[0, t].astype(jnp.float32)
        wbuf[:, t * TLON:(t + 1) * TLON] = jnp.full((ROWS, TLON), flag, jnp.float32)

    @pl.when(lat == 0)
    def _():
        for k in range(STEPS):
            row_in[k, 1] = jnp.zeros(row_in.shape[2:], jnp.float32)

    lane = lax.broadcasted_iota(jnp.int32, (ROWS, LANES), 1)

    def remote(src, dst, send, recv, device_id):
        return pltpu.make_async_remote_copy(
            src_ref=src, dst_ref=dst, send_sem=send, recv_sem=recv,
            device_id=device_id, device_id_type=MESH,
        )

    def copies(k):
        return (
            remote(col_out.at[k, 0], col_in.at[k, 0], send_sem.at[k, 0], recv_sem.at[k, 0], {"lon": west}),
            remote(col_out.at[k, 1], col_in.at[k, 1], send_sem.at[k, 1], recv_sem.at[k, 1], {"lon": east}),
            remote(row_out.at[k, 0], row_in.at[k, 0], send_sem.at[k, 2], recv_sem.at[k, 2], {"lat": lat - 1}),
            remote(row_out.at[k, 1], row_in.at[k, 1], send_sem.at[k, 3], recv_sem.at[k, 3], {"lat": lat + 1}),
            remote(row_out.at[k, 2], row_in.at[k, 0], send_sem.at[k, 4], recv_sem.at[k, 2], {"lon": mirror}),
        )

    def send_edges(k, src, state, first):
        to_west, to_east, to_south, to_north, to_mirror = copies(k)
        for l in range(levels):
            x = src[l, 0:1, :]
            y = src[l, height - 1:height, :]
            if first:
                x = x * wbuf[0:1, :]
                y = y * wbuf[0:1, :]
            vx = advect_scale * v[state, l, 0:1, :]
            vy = advect_scale * v[state, l, height - 1:height, :]
            dy = dv[height - 1:height, :]
            row_out[k, 0, l:l + 1, :] = (dv[0:1, :] + vx) * x
            row_out[k, 1, l:l + 1, :] = (dy - vy) * y
            row_out[k, 2, l:l + 1, :] = (dy + vy) * y

        @pl.when(lat > 0)
        def _():
            to_south.start()

        @pl.when(lat < top)
        def _():
            to_north.start()

        @pl.when(lat == top)
        def _():
            rows = row_out[k, 2]
            padded = rows.shape[0]
            parts = []
            for r in range(padded // ROWS):
                parts.append([
                    jnp.take_along_axis(
                        rows[r * ROWS:(r + 1) * ROWS, t * LANES:(t + 1) * LANES],
                        LANES - 1 - lane, axis=1)
                    for t in range(width // LANES)
                ])
            for r, tiles in enumerate(parts):
                for t, tile in enumerate(tiles):
                    place = width // LANES - 1 - t
                    row_out[k, 2, r * ROWS:(r + 1) * ROWS, place * LANES:(place + 1) * LANES] = tile
            to_mirror.start()

        def pack(j, packed):
            low, high = packed
            rows = pl.ds(pl.multiple_of(j * ROWS, ROWS), ROWS)
            for l in range(levels):
                here = lane == j * pitch + l
                x = src[l, rows, 0:LANES]
                y = src[l, rows, width - LANES:width]
                if first:
                    x = x * wbuf[:, 0:LANES]
                    y = y * wbuf[:, width - LANES:width]
                x = (dv[rows, 0:LANES] + advect_scale * u[state, l, rows, 0:LANES]) * x
                y = (dv[rows, width - LANES:width] - advect_scale * u[state, l, rows, width - LANES:width]) * y
                low = jnp.where(here, jnp.broadcast_to(x[:, 0:1], (ROWS, LANES)), low)
                high = jnp.where(here, jnp.broadcast_to(y[:, LANES - 1:LANES], (ROWS, LANES)), high)
            return low, high

        zero = jnp.zeros((ROWS, LANES), jnp.float32)
        low, high = lax.fori_loop(0, strips, pack, (zero, zero))
        col_out[k, 0] = low
        col_out[k, 1] = high
        to_west.start()
        to_east.start()

    def vertical(src, dst, first):
        def strip(j, _):
            rows = pl.ds(pl.multiple_of(j * ROWS, ROWS), ROWS)
            for t in range(width // LANES):
                cols = slice(t * LANES, (t + 1) * LANES)
                xs = [src[m, rows, cols] for m in range(levels)]
                if first:
                    xs = [x * wbuf[:, cols] for x in xs]
                for l in range(levels):
                    total = xs[0] * mix[0, l]
                    for m in range(1, levels):
                        total = total + xs[m] * mix[m, l]
                    dst[l, rows, cols] = total
            return 0

        lax.fori_loop(0, strips, strip, 0)

    def horizontal(src, dst, state, first):
        row = lax.broadcasted_iota(jnp.int32, (height, width), 0)
        column = lax.broadcasted_iota(jnp.int32, (height, width), 1)

        def level(l, _):
            w = jnp.broadcast_to(wbuf[0:1, :], (height, width))
            x = src[l]
            if first:
                x = x * w
            d = dv[...]
            zonal = advect_scale * u[state, l]
            merid = advect_scale * v[state, l]
            tracer = q[state, l]
            total = dst[l] + x * (1.0 - 4.0 * d - damping * tracer * tracer)
            total += jnp.where(column == width - 1, 0.0, pltpu.roll((d + zonal) * x, width - 1, 1))
            total += jnp.where(column == 0, 0.0, pltpu.roll((d - zonal) * x, 1, 1))
            total += jnp.where(row == height - 1, 0.0, pltpu.roll((d + merid) * x, height - 1, 0))
            total += jnp.where(row == 0, 0.0, pltpu.roll((d - merid) * x, 1, 0))
            dst[l] = w * total
            return 0

        lax.fori_loop(0, levels, level, 0)

    def add_edges(k, dst):
        from_east, from_west, from_north, from_south, _ = copies(k)
        from_north.wait_recv()

        @pl.when(lat > 0)
        def _():
            from_south.wait_recv()

        w = wbuf[0:1, :]
        for l in range(levels):
            dst[l, height - 1:height, :] = dst[l, height - 1:height, :] + w * row_in[k, 0, l:l + 1, :]
            dst[l, 0:1, :] = dst[l, 0:1, :] + w * row_in[k, 1, l:l + 1, :]
        from_east.wait_recv()
        from_west.wait_recv()
        high = col_in[k, 0] * wbuf[:, width - LANES:width]
        low = col_in[k, 1] * wbuf[:, 0:LANES]

        def unpack(j, _):
            rows = pl.ds(pl.multiple_of(j * ROWS, ROWS), ROWS)
            shift = lax.rem(LANES - j * pitch, LANES)
            h = pltpu.roll(high, shift, 1)
            g = pltpu.roll(low, shift, 1)
            for l in range(levels):
                hl = jnp.broadcast_to(h[:, l:l + 1], (ROWS, LANES))
                gl = jnp.broadcast_to(g[:, l:l + 1], (ROWS, LANES))
                cols = slice(width - LANES, width)
                dst[l, rows, cols] = dst[l, rows, cols] + jnp.where(lane == LANES - 1, hl, 0.0)
                cols = slice(0, LANES)
                dst[l, rows, cols] = dst[l, rows, cols] + jnp.where(lane == 0, gl, 0.0)
            return 0

        lax.fori_loop(0, strips, unpack, 0)

    def finish_sends(k):
        to_west, to_east, to_south, to_north, to_mirror = copies(k)
        to_west.wait_send()
        to_east.wait_send()

        @pl.when(lat > 0)
        def _():
            to_south.wait_send()

        @pl.when(lat < top)
        def _():
            to_north.wait_send()

        @pl.when(lat == top)
        def _():
            to_mirror.wait_send()

    for load in loads[:2 + 2 * store]:
        load.wait()

    @pl.when(four)
    def _():
        pl.semaphore_wait(barrier, 4)

    @pl.when(jnp.logical_not(four))
    def _():
        pl.semaphore_wait(barrier, 3)

    state = sidx[STEPS - 1]
    send_edges(0, af, state, True)
    vertical(af, mid, True)
    for load in loads[2 + 2 * store:]:
        load.wait()
    horizontal(af, mid, state, True)
    add_edges(0, mid)

    state = sidx[STEPS - 2]
    send_edges(1, mid, state, False)
    vertical(mid, out, False)
    horizontal(mid, out, state, False)
    add_edges(1, out)
    finish_sends(0)
    finish_sends(1)


def shards(lons, lats, af, q, u, v, d, mix, wet, sidx):
    levels, height, width = af.shape
    store = u.shape[0]
    padded = -(-levels // ROWS) * ROWS
    f32 = jnp.float32
    hbm = pl.BlockSpec(memory_space=pltpu.HBM)
    smem = pl.BlockSpec(memory_space=pltpu.SMEM)
    vmem = pl.BlockSpec(memory_space=pltpu.VMEM)
    cells = levels * height * width
    return pl.pallas_call(
        functools.partial(kernel, lons, lats),
        out_shape=jax.ShapeDtypeStruct((levels, height, width), f32),
        in_specs=[hbm] * 5 + [smem] * 3,
        out_specs=vmem,
        scratch_shapes=[
            pltpu.VMEM((levels, height, width), f32),
            pltpu.VMEM((store, levels, height, width), f32),
            pltpu.VMEM((store, levels, height, width), f32),
            pltpu.VMEM((store, levels, height, width), f32),
            pltpu.VMEM((height, width), f32),
            pltpu.VMEM((levels, height, width), f32),
            pltpu.VMEM((ROWS, width), f32),
            pltpu.VMEM((STEPS, 2, ROWS, LANES), f32),
            pltpu.VMEM((STEPS, 2, ROWS, LANES), f32),
            pltpu.VMEM((STEPS, 3, padded, width), f32),
            pltpu.VMEM((STEPS, 2, padded, width), f32),
            pltpu.SemaphoreType.DMA((2 + 3 * store,)),
            pltpu.SemaphoreType.DMA((STEPS, 5)),
            pltpu.SemaphoreType.DMA((STEPS, 4)),
        ],
        compiler_params=pltpu.CompilerParams(
            collective_id=0, has_side_effects=True, vmem_limit_bytes=56 * 1024 * 1024
        ),
        cost_estimate=pl.CostEstimate(
            flops=90 * cells, bytes_accessed=4 * cells * (3 * store + 2), transcendentals=0
        ),
    )(af, q, u, v, d, mix, wet, sidx)


def solution(mesh):
    return jax.shard_map(
        functools.partial(shards, mesh.shape["lon"], mesh.shape["lat"]),
        mesh=mesh,
        in_specs=(
            P(None, "lat", "lon"),
            P(None, None, "lat", "lon"),
            P(None, None, "lat", "lon"),
            P(None, None, "lat", "lon"),
            P("lat", "lon"),
            P(),
            P("lat", "lon"),
            P(),
        ),
        out_specs=P(None, "lat", "lon"),
        check_vma=False,
    )
```

```python
import functools

import jax
import jax.numpy as jnp
from jax import lax
from jax.experimental import pallas as pl
from jax.experimental.pallas import tpu as pltpu
from jax.sharding import PartitionSpec as P

TLON = 128
STEPS = 2
LANES = 128
ROWS = 8

advect_scale = 0.25
damping = 0.3

MESH = pl.DeviceIdType.MESH


def kernel(
    lons, lats,
    af_h, q_h, u_h, v_h, d_h, mix, wet, sidx,
    out,
    af, q, u, v, dv, mid, wbuf, col_out, col_in, row_out, row_in,
    load_sem, send_sem, recv_sem,
):
    levels, height, width = af.shape
    store = u.shape[0]
    strips = height // ROWS
    pitch = LANES // strips
    padded = row_in.shape[2] - ROWS
    lon = lax.axis_index("lon")
    lat = lax.axis_index("lat")
    east = lax.rem(lon + 1, lons)
    west = lax.rem(lon + lons - 1, lons)
    mirror = lons - 1 - lon
    top = lats - 1

    barrier = pltpu.get_barrier_semaphore()

    def greet(device_id):
        pl.semaphore_signal(barrier, inc=1, device_id=device_id, device_id_type=MESH)

    greet({"lon": east})
    greet({"lon": west})

    @pl.when(lat < top)
    def _():
        greet({"lat": lat + 1})

    folds = (lat == top) & (mirror != east) & (mirror != west)
    four = ((lat > 0) & (lat < top)) | folds

    @pl.when(folds)
    def _():
        greet({"lon": mirror})

    @pl.when(lat > 0)
    def _():
        greet({"lat": lat - 1})

    loads = [(d_h, dv), (af_h, af)]
    loads += [(u_h.at[s], u.at[s]) for s in range(store)]
    loads += [(v_h.at[s], v.at[s]) for s in range(store)]
    loads += [(q_h.at[s], q.at[s]) for s in range(store)]
    loads = [pltpu.make_async_copy(src, dst, load_sem.at[i]) for i, (src, dst) in enumerate(loads)]
    early = loads[:2 + store]
    for load in early:
        load.start()

    for t in range(width // TLON):
        flag = wet[0, t].astype(jnp.float32)
        wbuf[:, t * TLON:(t + 1) * TLON] = jnp.full((ROWS, TLON), flag, jnp.float32)

    @pl.when(lat == 0)
    def _():
        for k in range(STEPS):
            row_in[k, 1] = jnp.zeros(row_in.shape[2:], jnp.float32)

    lane = lax.broadcasted_iota(jnp.int32, (ROWS, LANES), 1)
    sublane = lax.broadcasted_iota(jnp.int32, (ROWS, LANES), 0)

    def remote(src, dst, send, recv, device_id):
        return pltpu.make_async_remote_copy(
            src_ref=src, dst_ref=dst, send_sem=send, recv_sem=recv,
            device_id=device_id, device_id_type=MESH,
        )

    def copies(k):
        return (
            remote(col_out.at[k, 0], col_in.at[k, 0], send_sem.at[k, 0], recv_sem.at[k, 0], {"lon": west}),
            remote(col_out.at[k, 1], col_in.at[k, 1], send_sem.at[k, 1], recv_sem.at[k, 1], {"lon": east}),
            remote(row_out.at[k, 0], row_in.at[k, 0], send_sem.at[k, 2], recv_sem.at[k, 2], {"lat": lat - 1}),
            remote(row_out.at[k, 1], row_in.at[k, 1], send_sem.at[k, 3], recv_sem.at[k, 3], {"lat": lat + 1}),
            remote(row_out.at[k, 2], row_in.at[k, 0], send_sem.at[k, 4], recv_sem.at[k, 2], {"lon": mirror}),
        )

    def pack(column):
        packed = jnp.zeros((ROWS, LANES), jnp.float32)
        for j in range(strips):
            for l in range(levels):
                tile, place = column(l, slice(j * ROWS, (j + 1) * ROWS))
                spread = jnp.broadcast_to(tile[:, place:place + 1], (ROWS, LANES))
                packed = jnp.where(lane == j * pitch + l, spread, packed)
        return packed,

    def west_flux(state, apply):
        def column(l, rows):
            rate = dv[rows, 0:LANES] + advect_scale * u[state, l, rows, 0:LANES]
            if apply:
                rate = rate * (af[l, rows, 0:LANES] * wbuf[:, 0:LANES])
            return rate, 0
        return column

    def east_flux(state, apply):
        cols = slice(width - LANES, width)

        def column(l, rows):
            rate = dv[rows, cols] - advect_scale * u[state, l, rows, cols]
            if apply:
                rate = rate * (af[l, rows, cols] * wbuf[:, cols])
            return rate, LANES - 1
        return column

    def send_columns(k, low, high):
        to_west, to_east, *_ = copies(k)
        col_out[k, 0] = low
        col_out[k, 1] = high
        to_west.start()
        to_east.start()

    def corner_rows(k, slot, strip, r, swap):
        low = jnp.zeros((ROWS, LANES), jnp.float32)
        high = low
        for l in range(levels):
            here = (lane == strip * pitch + l) & (sublane == r)
            x = jnp.broadcast_to(row_out[k, slot, l:l + 1, 0:LANES][:, 0:1], (ROWS, LANES))
            y = jnp.broadcast_to(row_out[k, slot, l:l + 1, width - LANES:width][:, LANES - 1:LANES], (ROWS, LANES))
            low = jnp.where(here, x, low)
            high = jnp.where(here, y, high)
        if swap:
            low, high = high, low
        row_out[k, slot, padded:padded + ROWS, 0:LANES] = low
        row_out[k, slot, padded:padded + ROWS, width - LANES:width] = high

    def send_rows(k, src, state, first):
        _, _, to_south, to_north, to_mirror = copies(k)
        for l in range(levels):
            x = src[l, 0:1, :]
            y = src[l, height - 1:height, :]
            if first:
                x = x * wbuf[0:1, :]
                y = y * wbuf[0:1, :]
            vx = advect_scale * v[state, l, 0:1, :]
            vy = advect_scale * v[state, l, height - 1:height, :]
            dy = dv[height - 1:height, :]
            row_out[k, 0, l:l + 1, :] = (dv[0:1, :] + vx) * x
            row_out[k, 1, l:l + 1, :] = (dy - vy) * y
            row_out[k, 2, l:l + 1, :] = (dy + vy) * y

        if first:
            corner_rows(k, 0, strips - 1, ROWS - 1, False)
            corner_rows(k, 1, 0, 0, False)

        @pl.when(lat > 0)
        def _():
            to_south.start()

        @pl.when(lat < top)
        def _():
            to_north.start()

        @pl.when(lat == top)
        def _():
            if first:
                corner_rows(k, 2, strips - 1, ROWS - 1, True)
            rows = row_out[k, 2, 0:padded, :]
            parts = []
            for r in range(padded // ROWS):
                parts.append([
                    jnp.take_along_axis(
                        rows[r * ROWS:(r + 1) * ROWS, t * LANES:(t + 1) * LANES],
                        LANES - 1 - lane, axis=1)
                    for t in range(width // LANES)
                ])
            for r, tiles in enumerate(parts):
                for t, tile in enumerate(tiles):
                    place = width // LANES - 1 - t
                    row_out[k, 2, r * ROWS:(r + 1) * ROWS, place * LANES:(place + 1) * LANES] = tile
            to_mirror.start()

    def vertical(src, dst, first):
        def strip(j, _):
            rows = pl.ds(pl.multiple_of(j * ROWS, ROWS), ROWS)
            for t in range(width // LANES):
                cols = slice(t * LANES, (t + 1) * LANES)
                xs = [src[m, rows, cols] for m in range(levels)]
                if first:
                    xs = [x * wbuf[:, cols] for x in xs]
                for l in range(levels):
                    total = xs[0] * mix[0, l]
                    for m in range(1, levels):
                        total = total + xs[m] * mix[m, l]
                    dst[l, rows, cols] = total
            return 0

        lax.fori_loop(0, strips, strip, 0, unroll=True)

    def horizontal(src, dst, state, first):
        row = lax.broadcasted_iota(jnp.int32, (height, width), 0)
        column = lax.broadcasted_iota(jnp.int32, (height, width), 1)

        def level(l, _):
            w = jnp.broadcast_to(wbuf[0:1, :], (height, width))
            x = src[l]
            if first:
                x = x * w
            d = dv[...]
            zonal = advect_scale * u[state, l]
            merid = advect_scale * v[state, l]
            tracer = q[state, l]
            total = dst[l] + x * (1.0 - 4.0 * d - damping * tracer * tracer)
            total += jnp.where(column == width - 1, 0.0, pltpu.roll((d + zonal) * x, width - 1, 1))
            total += jnp.where(column == 0, 0.0, pltpu.roll((d - zonal) * x, 1, 1))
            total += jnp.where(row == height - 1, 0.0, pltpu.roll((d + merid) * x, height - 1, 0))
            total += jnp.where(row == 0, 0.0, pltpu.roll((d - merid) * x, 1, 0))
            dst[l] = w * total
            return 0

        lax.fori_loop(0, levels, level, 0, unroll=True)

    def wait_edges(k):
        from_east, from_west, from_north, from_south, _ = copies(k)
        from_north.wait_recv()

        @pl.when(lat > 0)
        def _():
            from_south.wait_recv()

        from_east.wait_recv()
        from_west.wait_recv()

    def add_edges(k, dst):
        w = wbuf[0:1, :]
        for l in range(levels):
            dst[l, height - 1:height, :] = dst[l, height - 1:height, :] + w * row_in[k, 0, l:l + 1, :]
            dst[l, 0:1, :] = dst[l, 0:1, :] + w * row_in[k, 1, l:l + 1, :]
        high = col_in[k, 0] * wbuf[:, width - LANES:width]
        low = col_in[k, 1] * wbuf[:, 0:LANES]
        first_cols = slice(0, LANES)
        last_cols = slice(width - LANES, width)
        for j in range(strips):
            rows = slice(j * ROWS, (j + 1) * ROWS)
            news = []
            for l in range(levels):
                at = j * pitch + l
                g = jnp.broadcast_to(low[:, at:at + 1], (ROWS, LANES))
                h = jnp.broadcast_to(high[:, at:at + 1], (ROWS, LANES))
                news.append((
                    dst[l, rows, first_cols] + jnp.where(lane == 0, g, 0.0),
                    dst[l, rows, last_cols] + jnp.where(lane == LANES - 1, h, 0.0)))
            for l, (g, h) in enumerate(news):
                dst[l, rows, first_cols] = g
                dst[l, rows, last_cols] = h

    def finish_sends(k):
        to_west, to_east, to_south, to_north, to_mirror = copies(k)
        to_west.wait_send()
        to_east.wait_send()

        @pl.when(lat > 0)
        def _():
            to_south.wait_send()

        @pl.when(lat < top)
        def _():
            to_north.wait_send()

        @pl.when(lat == top)
        def _():
            to_mirror.wait_send()

    for load in early:
        load.wait()
    for load in loads[2 + store:]:
        load.start()

    @pl.when(four)
    def _():
        pl.semaphore_wait(barrier, 4)

    @pl.when(jnp.logical_not(four))
    def _():
        pl.semaphore_wait(barrier, 3)

    first = sidx[STEPS - 1]
    second = sidx[STEPS - 2]
    send_columns(0, *pack(west_flux(first, True)), *pack(east_flux(first, True)))
    for load in loads[2 + store:2 + 2 * store]:
        load.wait()
    send_rows(0, af, first, True)
    vertical(af, mid, True)
    for load in loads[2 + 2 * store:]:
        load.wait()
    horizontal(af, mid, first, True)

    low_part, = pack(lambda l, rows: (mid[l, rows, 0:LANES], 0))
    high_part, = pack(lambda l, rows: (mid[l, rows, width - LANES:width], LANES - 1))
    low_rate, = pack(west_flux(second, False))
    high_rate, = pack(east_flux(second, False))
    wait_edges(0)
    corners = row_in[0, 0, padded:padded + ROWS, :] + row_in[0, 1, padded:padded + ROWS, :]
    low_part += wbuf[:, 0:LANES] * (col_in[0, 1] + corners[:, 0:LANES])
    high_part += wbuf[:, width - LANES:width] * (col_in[0, 0] + corners[:, width - LANES:width])
    send_columns(1, low_rate * low_part, high_rate * high_part)
    add_edges(0, mid)
    send_rows(1, mid, second, False)
    vertical(mid, out, False)
    horizontal(mid, out, second, False)
    wait_edges(1)
    add_edges(1, out)
    finish_sends(0)
    finish_sends(1)


def shards(lons, lats, af, q, u, v, d, mix, wet, sidx):
    levels, height, width = af.shape
    store = u.shape[0]
    padded = -(-levels // ROWS) * ROWS
    f32 = jnp.float32
    hbm = pl.BlockSpec(memory_space=pltpu.HBM)
    smem = pl.BlockSpec(memory_space=pltpu.SMEM)
    vmem = pl.BlockSpec(memory_space=pltpu.VMEM)
    cells = levels * height * width
    return pl.pallas_call(
        functools.partial(kernel, lons, lats),
        out_shape=pltpu.VMEM((levels, height, width), f32),
        in_specs=[hbm] * 5 + [smem] * 3,
        out_specs=vmem,
        scratch_shapes=[
            pltpu.VMEM((levels, height, width), f32),
            pltpu.VMEM((store, levels, height, width), f32),
            pltpu.VMEM((store, levels, height, width), f32),
            pltpu.VMEM((store, levels, height, width), f32),
            pltpu.VMEM((height, width), f32),
            pltpu.VMEM((levels, height, width), f32),
            pltpu.VMEM((ROWS, width), f32),
            pltpu.VMEM((STEPS, 2, ROWS, LANES), f32),
            pltpu.VMEM((STEPS, 2, ROWS, LANES), f32),
            pltpu.VMEM((STEPS, 3, padded + ROWS, width), f32),
            pltpu.VMEM((STEPS, 2, padded + ROWS, width), f32),
            pltpu.SemaphoreType.DMA((2 + 3 * store,)),
            pltpu.SemaphoreType.DMA((STEPS, 5)),
            pltpu.SemaphoreType.DMA((STEPS, 4)),
        ],
        compiler_params=pltpu.CompilerParams(
            collective_id=0, has_side_effects=True, vmem_limit_bytes=56 * 1024 * 1024
        ),
        cost_estimate=pl.CostEstimate(
            flops=90 * cells, bytes_accessed=4 * cells * (3 * store + 2), transcendentals=0
        ),
    )(af, q, u, v, d, mix, wet, sidx)


def solution(mesh):
    return jax.shard_map(
        functools.partial(shards, mesh.shape["lon"], mesh.shape["lat"]),
        mesh=mesh,
        in_specs=(
            P(None, "lat", "lon"),
            P(None, None, "lat", "lon"),
            P(None, None, "lat", "lon"),
            P(None, None, "lat", "lon"),
            P("lat", "lon"),
            P(),
            P("lat", "lon"),
            P(),
        ),
        out_specs=P(None, "lat", "lon"),
        check_vma=False,
    )
```

```python
import functools

import jax
import jax.numpy as jnp
from jax import lax
from jax.experimental import pallas as pl
from jax.experimental.pallas import tpu as pltpu
from jax.sharding import PartitionSpec as P

TLON = 128
STEPS = 2
LANES = 128
ROWS = 8

advect_scale = 0.25
damping = 0.3

MESH = pl.DeviceIdType.MESH


def kernel(
    lons, lats,
    af_h, q_h, u_h, v_h, d_h, mix, wet, sidx,
    out,
    af, q, u, v, dv, mid, wbuf, col_out, col_in, row_out, row_in,
    load_sem, send_sem, recv_sem,
):
    levels, height, width = af.shape
    store = u.shape[0]
    strips = height // ROWS
    pitch = LANES // strips
    padded = row_in.shape[2] - ROWS
    lon = lax.axis_index("lon")
    lat = lax.axis_index("lat")
    east = lax.rem(lon + 1, lons)
    west = lax.rem(lon + lons - 1, lons)
    mirror = lons - 1 - lon
    top = lats - 1

    barrier = pltpu.get_barrier_semaphore()

    def greet(device_id):
        pl.semaphore_signal(barrier, inc=1, device_id=device_id, device_id_type=MESH)

    greet({"lon": east})
    greet({"lon": west})

    @pl.when(lat < top)
    def _():
        greet({"lat": lat + 1})

    folds = (lat == top) & (mirror != east) & (mirror != west)
    four = ((lat > 0) & (lat < top)) | folds

    @pl.when(folds)
    def _():
        greet({"lon": mirror})

    @pl.when(lat > 0)
    def _():
        greet({"lat": lat - 1})

    loads = [(d_h, dv), (af_h, af)]
    loads += [(u_h.at[s], u.at[s]) for s in range(store)]
    loads += [(v_h.at[s], v.at[s]) for s in range(store)]
    loads += [(q_h.at[s], q.at[s]) for s in range(store)]
    loads = [pltpu.make_async_copy(src, dst, load_sem.at[i]) for i, (src, dst) in enumerate(loads)]
    early = loads[:2 + store]
    for load in early:
        load.start()

    for t in range(width // TLON):
        flag = wet[0, t].astype(jnp.float32)
        wbuf[:, t * TLON:(t + 1) * TLON] = jnp.full((ROWS, TLON), flag, jnp.float32)

    @pl.when(lat == 0)
    def _():
        for k in range(STEPS):
            row_in[k, 1] = jnp.zeros(row_in.shape[2:], jnp.float32)

    lane = lax.broadcasted_iota(jnp.int32, (ROWS, LANES), 1)
    sublane = lax.broadcasted_iota(jnp.int32, (ROWS, LANES), 0)

    def remote(src, dst, send, recv, device_id):
        return pltpu.make_async_remote_copy(
            src_ref=src, dst_ref=dst, send_sem=send, recv_sem=recv,
            device_id=device_id, device_id_type=MESH,
        )

    def copies(k):
        return (
            remote(col_out.at[k, 0], col_in.at[k, 0], send_sem.at[k, 0], recv_sem.at[k, 0], {"lon": west}),
            remote(col_out.at[k, 1], col_in.at[k, 1], send_sem.at[k, 1], recv_sem.at[k, 1], {"lon": east}),
            remote(row_out.at[k, 0], row_in.at[k, 0], send_sem.at[k, 2], recv_sem.at[k, 2], {"lat": lat - 1}),
            remote(row_out.at[k, 1], row_in.at[k, 1], send_sem.at[k, 3], recv_sem.at[k, 3], {"lat": lat + 1}),
            remote(row_out.at[k, 2], row_in.at[k, 0], send_sem.at[k, 4], recv_sem.at[k, 2], {"lon": mirror}),
        )

    def pack(column):
        packed = jnp.zeros((ROWS, LANES), jnp.float32)
        for j in range(strips):
            for l in range(levels):
                tile, place = column(l, slice(j * ROWS, (j + 1) * ROWS))
                spread = jnp.broadcast_to(tile[:, place:place + 1], (ROWS, LANES))
                packed = jnp.where(lane == j * pitch + l, spread, packed)
        return packed,

    def west_flux(state, apply):
        def column(l, rows):
            rate = dv[rows, 0:LANES] + advect_scale * u[state, l, rows, 0:LANES]
            if apply:
                rate = rate * (af[l, rows, 0:LANES] * wbuf[:, 0:LANES])
            return rate, 0
        return column

    def east_flux(state, apply):
        cols = slice(width - LANES, width)

        def column(l, rows):
            rate = dv[rows, cols] - advect_scale * u[state, l, rows, cols]
            if apply:
                rate = rate * (af[l, rows, cols] * wbuf[:, cols])
            return rate, LANES - 1
        return column

    def send_columns(k, low, high):
        to_west, to_east, *_ = copies(k)
        col_out[k, 0] = low
        col_out[k, 1] = high
        to_west.start()
        to_east.start()

    def corner_rows(k, slot, strip, r, swap):
        low = jnp.zeros((ROWS, LANES), jnp.float32)
        high = low
        for l in range(levels):
            here = (lane == strip * pitch + l) & (sublane == r)
            x = jnp.broadcast_to(row_out[k, slot, l:l + 1, 0:LANES][:, 0:1], (ROWS, LANES))
            y = jnp.broadcast_to(row_out[k, slot, l:l + 1, width - LANES:width][:, LANES - 1:LANES], (ROWS, LANES))
            low = jnp.where(here, x, low)
            high = jnp.where(here, y, high)
        if swap:
            low, high = high, low
        row_out[k, slot, padded:padded + ROWS, 0:LANES] = low
        row_out[k, slot, padded:padded + ROWS, width - LANES:width] = high

    def send_rows(k, src, state, first):
        _, _, to_south, to_north, to_mirror = copies(k)
        for l in range(levels):
            x = src[l, 0:1, :]
            y = src[l, height - 1:height, :]
            if first:
                x = x * wbuf[0:1, :]
                y = y * wbuf[0:1, :]
            vx = advect_scale * v[state, l, 0:1, :]
            vy = advect_scale * v[state, l, height - 1:height, :]
            dy = dv[height - 1:height, :]
            row_out[k, 0, l:l + 1, :] = (dv[0:1, :] + vx) * x
            row_out[k, 1, l:l + 1, :] = (dy - vy) * y
            row_out[k, 2, l:l + 1, :] = (dy + vy) * y

        if first:
            corner_rows(k, 0, strips - 1, ROWS - 1, False)
            corner_rows(k, 1, 0, 0, False)

        @pl.when(lat > 0)
        def _():
            to_south.start()

        @pl.when(lat < top)
        def _():
            to_north.start()

        @pl.when(lat == top)
        def _():
            if first:
                corner_rows(k, 2, strips - 1, ROWS - 1, True)
            rows = row_out[k, 2, 0:padded, :]
            parts = []
            for r in range(padded // ROWS):
                parts.append([
                    jnp.take_along_axis(
                        rows[r * ROWS:(r + 1) * ROWS, t * LANES:(t + 1) * LANES],
                        LANES - 1 - lane, axis=1)
                    for t in range(width // LANES)
                ])
            for r, tiles in enumerate(parts):
                for t, tile in enumerate(tiles):
                    place = width // LANES - 1 - t
                    row_out[k, 2, r * ROWS:(r + 1) * ROWS, place * LANES:(place + 1) * LANES] = tile
            to_mirror.start()

    def vertical(src, dst, first):
        def strip(j, _):
            rows = pl.ds(pl.multiple_of(j * ROWS, ROWS), ROWS)
            for t in range(width // LANES):
                cols = slice(t * LANES, (t + 1) * LANES)
                xs = [src[m, rows, cols] for m in range(levels)]
                if first:
                    xs = [x * wbuf[:, cols] for x in xs]
                for l in range(levels):
                    total = xs[0] * mix[0, l]
                    for m in range(1, levels):
                        total = total + xs[m] * mix[m, l]
                    dst[l, rows, cols] = total
            return 0

        lax.fori_loop(0, strips, strip, 0, unroll=True)

    def horizontal(src, dst, state, first):
        row = lax.broadcasted_iota(jnp.int32, (height, width), 0)
        column = lax.broadcasted_iota(jnp.int32, (height, width), 1)

        def level(l, _):
            w = jnp.broadcast_to(wbuf[0:1, :], (height, width))
            x = src[l]
            if first:
                x = x * w
            d = dv[...]
            zonal = advect_scale * u[state, l]
            merid = advect_scale * v[state, l]
            tracer = q[state, l]
            total = dst[l] + x * (1.0 - 4.0 * d - damping * tracer * tracer)
            total += jnp.where(column == width - 1, 0.0, pltpu.roll((d + zonal) * x, width - 1, 1))
            total += jnp.where(column == 0, 0.0, pltpu.roll((d - zonal) * x, 1, 1))
            total += jnp.where(row == height - 1, 0.0, pltpu.roll((d + merid) * x, height - 1, 0))
            total += jnp.where(row == 0, 0.0, pltpu.roll((d - merid) * x, 1, 0))
            dst[l] = w * total
            return 0

        lax.fori_loop(0, levels, level, 0, unroll=True)

    def wait_rows(k):
        _, _, from_north, from_south, _ = copies(k)
        from_north.wait_recv()

        @pl.when(lat > 0)
        def _():
            from_south.wait_recv()

    def wait_columns(k):
        from_east, from_west, *_ = copies(k)
        from_east.wait_recv()
        from_west.wait_recv()

    def add_rows(k, dst):
        w = wbuf[0:1, :]
        for l in range(levels):
            dst[l, height - 1:height, :] = dst[l, height - 1:height, :] + w * row_in[k, 0, l:l + 1, :]
            dst[l, 0:1, :] = dst[l, 0:1, :] + w * row_in[k, 1, l:l + 1, :]

    def add_columns(k, dst):
        high = col_in[k, 0] * wbuf[:, width - LANES:width]
        low = col_in[k, 1] * wbuf[:, 0:LANES]
        first_cols = slice(0, LANES)
        last_cols = slice(width - LANES, width)
        for j in range(strips):
            rows = slice(j * ROWS, (j + 1) * ROWS)
            news = []
            for l in range(levels):
                at = j * pitch + l
                g = jnp.broadcast_to(low[:, at:at + 1], (ROWS, LANES))
                h = jnp.broadcast_to(high[:, at:at + 1], (ROWS, LANES))
                news.append((
                    dst[l, rows, first_cols] + jnp.where(lane == 0, g, 0.0),
                    dst[l, rows, last_cols] + jnp.where(lane == LANES - 1, h, 0.0)))
            for l, (g, h) in enumerate(news):
                dst[l, rows, first_cols] = g
                dst[l, rows, last_cols] = h

    def finish_sends(k):
        to_west, to_east, to_south, to_north, to_mirror = copies(k)
        to_west.wait_send()
        to_east.wait_send()

        @pl.when(lat > 0)
        def _():
            to_south.wait_send()

        @pl.when(lat < top)
        def _():
            to_north.wait_send()

        @pl.when(lat == top)
        def _():
            to_mirror.wait_send()

    for load in early:
        load.wait()
    for load in loads[2 + store:]:
        load.start()

    @pl.when(four)
    def _():
        pl.semaphore_wait(barrier, 4)

    @pl.when(jnp.logical_not(four))
    def _():
        pl.semaphore_wait(barrier, 3)

    first = sidx[STEPS - 1]
    second = sidx[STEPS - 2]
    send_columns(0, *pack(west_flux(first, True)), *pack(east_flux(first, True)))
    for load in loads[2 + store:2 + 2 * store]:
        load.wait()
    send_rows(0, af, first, True)
    vertical(af, mid, True)
    for load in loads[2 + 2 * store:]:
        load.wait()
    horizontal(af, mid, first, True)

    low_part, = pack(lambda l, rows: (mid[l, rows, 0:LANES], 0))
    high_part, = pack(lambda l, rows: (mid[l, rows, width - LANES:width], LANES - 1))
    low_rate, = pack(west_flux(second, False))
    high_rate, = pack(east_flux(second, False))
    wait_rows(0)
    corners = row_in[0, 0, padded:padded + ROWS, :] + row_in[0, 1, padded:padded + ROWS, :]
    low_part += wbuf[:, 0:LANES] * corners[:, 0:LANES]
    high_part += wbuf[:, width - LANES:width] * corners[:, width - LANES:width]
    add_rows(0, mid)
    wait_columns(0)
    low_part += wbuf[:, 0:LANES] * col_in[0, 1]
    high_part += wbuf[:, width - LANES:width] * col_in[0, 0]
    send_columns(1, low_rate * low_part, high_rate * high_part)
    add_columns(0, mid)
    send_rows(1, mid, second, False)
    vertical(mid, out, False)
    horizontal(mid, out, second, False)
    wait_rows(1)
    add_rows(1, out)
    finish_sends(0)
    wait_columns(1)
    add_columns(1, out)
    finish_sends(1)


def shards(lons, lats, af, q, u, v, d, mix, wet, sidx):
    levels, height, width = af.shape
    store = u.shape[0]
    padded = -(-levels // ROWS) * ROWS
    f32 = jnp.float32
    hbm = pl.BlockSpec(memory_space=pltpu.HBM)
    smem = pl.BlockSpec(memory_space=pltpu.SMEM)
    vmem = pl.BlockSpec(memory_space=pltpu.VMEM)
    cells = levels * height * width
    return pl.pallas_call(
        functools.partial(kernel, lons, lats),
        out_shape=pltpu.VMEM((levels, height, width), f32),
        in_specs=[hbm] * 5 + [smem] * 3,
        out_specs=vmem,
        scratch_shapes=[
            pltpu.VMEM((levels, height, width), f32),
            pltpu.VMEM((store, levels, height, width), f32),
            pltpu.VMEM((store, levels, height, width), f32),
            pltpu.VMEM((store, levels, height, width), f32),
            pltpu.VMEM((height, width), f32),
            pltpu.VMEM((levels, height, width), f32),
            pltpu.VMEM((ROWS, width), f32),
            pltpu.VMEM((STEPS, 2, ROWS, LANES), f32),
            pltpu.VMEM((STEPS, 2, ROWS, LANES), f32),
            pltpu.VMEM((STEPS, 3, padded + ROWS, width), f32),
            pltpu.VMEM((STEPS, 2, padded + ROWS, width), f32),
            pltpu.SemaphoreType.DMA((2 + 3 * store,)),
            pltpu.SemaphoreType.DMA((STEPS, 5)),
            pltpu.SemaphoreType.DMA((STEPS, 4)),
        ],
        compiler_params=pltpu.CompilerParams(
            collective_id=0, has_side_effects=True, vmem_limit_bytes=56 * 1024 * 1024
        ),
        cost_estimate=pl.CostEstimate(
            flops=90 * cells, bytes_accessed=4 * cells * (3 * store + 2), transcendentals=0
        ),
    )(af, q, u, v, d, mix, wet, sidx)


def solution(mesh):
    return jax.shard_map(
        functools.partial(shards, mesh.shape["lon"], mesh.shape["lat"]),
        mesh=mesh,
        in_specs=(
            P(None, "lat", "lon"),
            P(None, None, "lat", "lon"),
            P(None, None, "lat", "lon"),
            P(None, None, "lat", "lon"),
            P("lat", "lon"),
            P(),
            P("lat", "lon"),
            P(),
        ),
        out_specs=P(None, "lat", "lon"),
        check_vma=False,
    )
```
